512 devices in a mesh: dp: 8 (over x, z_hi), dap: 64 (over z_lo, y, core).
Axes of the slice: x: 4, y: 4, z: 16 (z_hi: 2, z_lo: 8; z = z_hi * 8 + z_lo), core: 2. Of those that a mesh axis runs over, the one named last changes fastest.
Arguments:
- alignment: bfloat16 [2048, 512, 256], P(('dp', 'dap')), parts along dimension 0, may hold values from -6 to 6
- pair_act: bfloat16 [4096, 512, 128], P(('dp', 'dap')), parts along dimension 0, may hold values from -6 to 6
- crop_mask: int32 [4096], P('dp'), parts along dimension 0, may hold values 0 or 1
- seq_mask: int32 [2048], P('dp'), parts along dimension 0, may hold values 0 or 1
- chain_ids: int32 [4096], P('dp'), parts along dimension 0, may hold values from 0 to 3, never falling along the last dimension, each value on 1 to 256 neighbouring positions
- chain_embed: float32 [2, 128], replicated, may hold values from -6 to 6
- score_proj: bfloat16 [2, 256, 256], replicated, may hold values from -40 to 40
- value_gate: bfloat16 [2, 256, 256], replicated, may hold values from -0.375 to 0.375
- column_out: bfloat16 [256, 256], replicated, may hold values from -0.375 to 0.375
- triangle_in: bfloat16 [2, 128, 640], replicated, may hold values from -0.5 to 0.5
- triangle_out: bfloat16 [2, 128, 128], replicated, may hold values from -0.5 to 0.5
Outputs:
- alignment_new: bfloat16 [2048, 512, 256], P('dp', 'dap'), parts along dimension 0
- pair_new: bfloat16 [4096, 512, 128], P(('dp', 'dap')), parts along dimension 0
The draws below stay inside these ranges and needn't reach their ends.
There are 8 independent parts, one for each index of `dp`. The reference program is written for one: setup_inputs(seed, part) draws one part's arguments, and reference() takes and returns one part's arrays. A program takes and returns all parts, laid end to end along the dimension named above; an argument that names none is the same for every part. Nothing has to cross between parts.
All inputs are finite; a program needn't handle non-finite values.
Results may differ from the reference program's by a relative error of at most 0.004.
The reference program's roundings to bfloat16 on the way count: a program that leaves them out, or rounds other values in their place, can miss the bound.
Values may be sent and summed in bfloat16 or wider, within the bound.
No kernel may reach another device: no remote copies, remote signals or barrier semaphores. Data moves between devices by JAX's collectives and lax.ppermute only.
A program may use at most 64 MiB of HBM per device.

```python
import math
import jax
import jax.numpy as jnp
import numpy as np
from jax import lax

CM = 256
CZ = 128
HEADS = 8
HEAD_DIM = 32
TC = 128
N_RES = 512
SEQS = 256


def draw_score_proj(key, part):
    key = jax.random.fold_in(key, 11)
    query_key, other_key = jax.random.split(key, 2)
    queries = jax.random.normal(query_key, (CM, HEADS * HEAD_DIM), jnp.float32) * CM ** (-0.5)
    others = jax.random.normal(other_key, (CM, HEADS * HEAD_DIM), jnp.float32) * CM ** (-0.5)
    key_rows = others
    return jnp.clip(jnp.stack([queries, key_rows]), -40.0, 40.0).astype(jnp.bfloat16)


def with_ends(values, stream_key, least, high):
    spot = [jax.random.randint(jax.random.fold_in(stream_key, axis), (), 0, length) for axis, length in enumerate(values.shape)]
    longest = values.shape.index(max(values.shape))
    beside = spot[:longest] + [(spot[longest] + 1) % values.shape[longest]] + spot[longest + 1:]
    return values.at[tuple(spot)].set(least).at[tuple(beside)].set(high)


def level_of(key, extent, pieces, least, high):
    gain, own = 1.0, jax.random.fold_in(key, 6)
    for dim, shards_of in pieces:
        heights = jnp.exp(jax.random.uniform(jax.random.fold_in(own, dim), (shards_of,), jnp.float32, least / len(pieces), high / len(pieces)))
        gain = gain * jnp.repeat(heights, extent[dim] // shards_of).reshape([-1 if axis == dim else 1 for axis in range(len(extent))])
    return gain


def length_profile(count, total, reach, skew):
    weights = [(1 << 20) // math.isqrt(standing ** skew) + 1 for standing in range(2, count + 1)]
    rest, holding = total - reach - (count - 1), [1] * (count - 1)
    while rest > 0:
        candidates = [i for i in range(count - 1) if holding[i] < reach]
        pool, remaining = sum([weights[i] for i in candidates]), rest
        for i in candidates:
            extra = min(reach - holding[i], max(1, remaining * weights[i] // pool), rest)
            holding[i] = holding[i] + extra
            rest = rest - extra
    return np.array([reach] + holding)


def ragged_sizes(stream_key, number_of, total, bound, lean):
    if number_of == 2:
        one = jax.random.randint(stream_key, (), max(1, total - bound), min(bound, total - 1) + 1)
        return jnp.stack([one, total - one])
    sizes = jnp.asarray(length_profile(number_of, total, bound, lean), jnp.int32)
    couples = (number_of - 1) // 2
    donor, receiver = sizes[1:1 + 2 * couples:2], sizes[2:2 + 2 * couples:2]
    slack = jnp.minimum(donor - 1, bound - receiver)
    shifted = jax.random.randint(jax.random.fold_in(stream_key, 1), (couples,), 0, 1 << 20) % (slack + 1)
    sizes = sizes.at[1:1 + 2 * couples:2].set(donor - shifted).at[2:2 + 2 * couples:2].set(receiver + shifted)
    return sizes[jax.random.permutation(jax.random.fold_in(stream_key, 2), number_of)]


def gaussian(stream_key, shape, spread, bound, cuts=(), kind=jnp.bfloat16):
    drawn = jax.random.normal(stream_key, shape, jnp.float32) * spread
    if len(cuts) > 0:
        drawn = level_of(stream_key, shape, cuts, -0.22, 0.18) * drawn
    return jnp.clip(drawn, min=-bound, max=bound).astype(kind)


def setup_inputs(seed: int = 0, part: int = 0) -> dict:
    splits = jax.random.split(jax.random.key(seed), 12)
    own_keys = jax.random.split(jax.random.fold_in(splits[11], part), 12)
    alignment = gaussian(own_keys[0], (SEQS, N_RES, CM), 1.0, 6.0, ((0, 64),))
    pair_act = gaussian(own_keys[1], (N_RES, N_RES, CZ), 1.0, 6.0, ((0, 64),))
    crop_mask = with_ends((jax.random.randint(own_keys[2], (N_RES,), 0, 8) < 7).astype(jnp.int32), jax.random.fold_in(own_keys[2], 1), 0, 1)
    seq_mask = with_ends((jax.random.randint(own_keys[3], (SEQS,), 0, 4) < 3).astype(jnp.int32), jax.random.fold_in(own_keys[3], 1), 0, 1)
    chain_ids = jnp.searchsorted(jnp.cumsum(ragged_sizes(own_keys[4], 4, N_RES, N_RES // 2, 0)), jnp.arange(N_RES), side="right").astype(jnp.int32)
    chain_embed = gaussian(splits[5], (2, CZ), 1.0, 6.0, (), jnp.float32)
    score_proj = draw_score_proj(jax.random.fold_in(splits[11], 71), part)
    value_gate = gaussian(splits[7], (2, CM, HEADS * HEAD_DIM), CM ** -0.5, 0.375)
    column_out = gaussian(splits[8], (HEADS * HEAD_DIM, CM), (HEADS * HEAD_DIM) ** -0.5, 0.375)
    triangle_in = gaussian(splits[9], (2, CZ, 4 * TC + CZ), CZ ** -0.5, 0.5)
    triangle_out = gaussian(splits[10], (2, TC, CZ), TC ** -0.5, 0.5)
    return dict(alignment=alignment, pair_act=pair_act, crop_mask=crop_mask, seq_mask=seq_mask, chain_ids=chain_ids, chain_embed=chain_embed, score_proj=score_proj, value_gate=value_gate, column_out=column_out, triangle_in=triangle_in, triangle_out=triangle_out)


EPS = 1e-05

def normalize(values, axis):
    average = lax.optimization_barrier(jnp.mean(values, axis=axis, keepdims=True))
    centered = values - average
    variance = lax.optimization_barrier(jnp.mean(centered * centered, axis=axis, keepdims=True))
    return centered * lax.rsqrt(variance + EPS)

def column_update(column, key_bias, score_proj, value_gate, column_out):
    count = column.shape[0]
    normed = normalize(column.astype(jnp.float32), 1).astype(jnp.bfloat16)
    queries = (jnp.dot(normed, score_proj[0], preferred_element_type=jnp.float32) * HEAD_DIM ** (-0.5)).astype(jnp.bfloat16)
    key_rows = jnp.dot(normed, score_proj[1], preferred_element_type=jnp.float32).astype(jnp.bfloat16)
    value_rows = jnp.dot(normed, value_gate[0], preferred_element_type=jnp.float32).astype(jnp.bfloat16)
    gate_rows = jax.nn.sigmoid(jnp.dot(normed, value_gate[1], preferred_element_type=jnp.float32))
    queries = queries.reshape(count, HEADS, HEAD_DIM).astype(jnp.float32)
    key_rows = key_rows.reshape(count, HEADS, HEAD_DIM).astype(jnp.float32)
    value_rows = value_rows.reshape(count, HEADS, HEAD_DIM).astype(jnp.float32)
    scores = jnp.einsum('shd,thd->hst', queries, key_rows) + key_bias[None, None, :]
    weights = jax.nn.softmax(scores, axis=-1).astype(jnp.bfloat16)
    mixture = jnp.einsum('hst,thd->shd', weights.astype(jnp.float32), value_rows).reshape(count, HEADS * HEAD_DIM)
    gated = (gate_rows * mixture).astype(jnp.bfloat16)
    return (column.astype(jnp.float32) + jnp.dot(gated, column_out, preferred_element_type=jnp.float32)).astype(jnp.bfloat16)

def triangle(pair_sum, pair_mask, weights_in, weights_out, incoming):
    width = weights_out.shape[0]
    side = pair_sum.shape[0]
    normed = normalize(pair_sum, 2).astype(jnp.bfloat16)
    projected = jnp.dot(normed.reshape(side * side, CZ), weights_in, preferred_element_type=jnp.float32).reshape(side, side, 4 * width + CZ)
    left_part = (jax.nn.sigmoid(projected[:, :, :width]) * projected[:, :, width:2 * width] * pair_mask[:, :, None]).astype(jnp.bfloat16)
    right_part = (jax.nn.sigmoid(projected[:, :, 2 * width:3 * width]) * projected[:, :, 3 * width:4 * width] * pair_mask[:, :, None]).astype(jnp.bfloat16)
    gate_part = jax.nn.sigmoid(projected[:, :, 4 * width:])
    if incoming:
        products = jnp.einsum('kic,kjc->ijc', left_part.astype(jnp.float32), right_part.astype(jnp.float32))
    else:
        products = jnp.einsum('ikc,jkc->ijc', left_part.astype(jnp.float32), right_part.astype(jnp.float32))
    products = products.astype(jnp.bfloat16)
    normed_products = normalize(products.astype(jnp.float32), 2).astype(jnp.bfloat16)
    update = jnp.dot(normed_products.reshape(side * side, width), weights_out, preferred_element_type=jnp.float32).reshape(side, side, CZ)
    return pair_sum + gate_part * update

def reference(alignment, pair_act, crop_mask, seq_mask, chain_ids, chain_embed, score_proj, value_gate, column_out, triangle_in, triangle_out):
    kept_rows = jnp.maximum(seq_mask, (jnp.arange(seq_mask.shape[0]) == 0).astype(jnp.int32))
    key_bias = (kept_rows - 1).astype(jnp.float32) * 1000000000.0
    by_column = jnp.moveaxis(alignment, 1, 0)
    attended = lax.map(lambda column: column_update(column, key_bias, score_proj, value_gate, column_out), by_column)
    alignment_new = jnp.moveaxis(attended, 0, 1)
    same_chain = chain_ids[:, None] == chain_ids[None, :]
    pair_sum = pair_act.astype(jnp.float32) + jnp.where(same_chain[:, :, None], chain_embed[0], chain_embed[1])
    crop = crop_mask.astype(jnp.float32)
    pair_mask = crop[:, None] * crop[None, :]
    pair_sum = triangle(pair_sum, pair_mask, triangle_in[0], triangle_out[0], False)
    pair_sum = triangle(pair_sum, pair_mask, triangle_in[1], triangle_out[1], True)
    return (alignment_new, pair_sum.astype(jnp.bfloat16))
```

```python
import functools

import jax
import jax.numpy as jnp
from jax import lax
from jax.sharding import PartitionSpec as P

HEADS = 8
HEAD_DIM = 32


EPS = 1e-05


def normalize(values, axis):
    average = jnp.mean(values, axis=axis, keepdims=True)
    centered = values - average
    variance = jnp.mean(centered * centered, axis=axis, keepdims=True)
    return centered * lax.rsqrt(variance + EPS)


def column_update(column, key_bias, score_proj, value_gate, column_out):
    count = column.shape[0]
    normed = normalize(column.astype(jnp.float32), 1).astype(jnp.bfloat16)
    queries = (
        jnp.dot(normed, score_proj[0], preferred_element_type=jnp.float32) * HEAD_DIM ** (-0.5)
    ).astype(jnp.bfloat16)
    key_rows = jnp.dot(normed, score_proj[1], preferred_element_type=jnp.float32).astype(
        jnp.bfloat16
    )
    value_rows = jnp.dot(normed, value_gate[0], preferred_element_type=jnp.float32).astype(
        jnp.bfloat16
    )
    gate_rows = jax.nn.sigmoid(jnp.dot(normed, value_gate[1], preferred_element_type=jnp.float32))
    queries = queries.reshape(count, HEADS, HEAD_DIM)
    key_rows = key_rows.reshape(count, HEADS, HEAD_DIM)
    value_rows = value_rows.reshape(count, HEADS, HEAD_DIM)
    scores = (
        jnp.einsum("shd,thd->hst", queries, key_rows, preferred_element_type=jnp.float32)
        + key_bias[None, None, :]
    )
    highest = jnp.max(scores, axis=-1, keepdims=True)
    raised = jnp.exp(scores - highest)
    weights = (raised / jnp.sum(raised, axis=-1, keepdims=True)).astype(jnp.bfloat16)
    mixture = jnp.einsum(
        "hst,thd->shd", weights, value_rows, preferred_element_type=jnp.float32
    ).reshape(count, HEADS * HEAD_DIM)
    gated = (gate_rows * mixture).astype(jnp.bfloat16)
    return (
        column.astype(jnp.float32) + jnp.dot(gated, column_out, preferred_element_type=jnp.float32)
    ).astype(jnp.bfloat16)


def project_pair(pair_sum, pair_mask, weights_in, width):
    normed = normalize(pair_sum, 2).astype(jnp.bfloat16)
    projected = jnp.einsum(
        "ijd,de->iej", normed, weights_in[:, : 4 * width], preferred_element_type=jnp.float32
    )
    left_part = (
        jax.nn.sigmoid(projected[:, :width])
        * projected[:, width : 2 * width]
        * pair_mask[:, None, :]
    ).astype(jnp.bfloat16)
    right_part = (
        jax.nn.sigmoid(projected[:, 2 * width : 3 * width])
        * projected[:, 3 * width : 4 * width]
        * pair_mask[:, None, :]
    ).astype(jnp.bfloat16)
    gate_part = jax.nn.sigmoid(
        jnp.einsum(
            "ijd,de->ije", normed, weights_in[:, 4 * width :], preferred_element_type=jnp.float32
        )
    )
    return (left_part, right_part, gate_part)


def exchange_parts(left_part, right_part):
    rows, width, side = left_part.shape
    devices = lax.axis_size("dap")
    share = width // devices
    both = jnp.concatenate(
        [part.reshape(rows, devices, share, side) for part in (left_part, right_part)], axis=2
    )
    both = lax.all_to_all(both, "dap", split_axis=1, concat_axis=0, tiled=True)
    both = both.reshape(rows * devices, 2 * share, side)
    return both


def return_products(products):
    return lax.all_to_all(products, "dap", split_axis=0, concat_axis=1, tiled=True)


def finish_triangle(pair_sum, products, gate_part, weights_out):
    normed_products = normalize(products.astype(jnp.float32), 1).astype(jnp.bfloat16)
    update = jnp.einsum(
        "icj,cd->ijd", normed_products, weights_out, preferred_element_type=jnp.float32
    )
    return pair_sum + gate_part * update


def on_device(
    alignment,
    pair_act,
    crop_mask,
    seq_mask,
    chain_ids,
    chain_embed,
    score_proj,
    value_gate,
    column_out,
    triangle_in,
    triangle_out,
):
    rows_here = pair_act.shape[0]
    width = triangle_out.shape[1]
    devices = lax.axis_size("dap")
    row_start = lax.axis_index("dap") * rows_here
    kept_rows = jnp.maximum(seq_mask, (jnp.arange(seq_mask.shape[0]) == 0).astype(jnp.int32))
    key_bias = (kept_rows - 1).astype(jnp.float32) * 1000000000.0
    crop = crop_mask.astype(jnp.float32)
    crop_rows = lax.dynamic_slice_in_dim(crop, row_start, rows_here)
    pair_mask = crop_rows[:, None] * crop[None, :]
    chain_rows = lax.dynamic_slice_in_dim(chain_ids, row_start, rows_here)
    same_chain = chain_rows[:, None] == chain_ids[None, :]
    pair_sum = pair_act.astype(jnp.float32) + jnp.where(
        same_chain[:, :, None], chain_embed[0], chain_embed[1]
    )
    seq_here = alignment.shape[0]
    blocked = alignment.reshape(seq_here, devices, rows_here, alignment.shape[2])
    blocked = lax.all_to_all(blocked, "dap", split_axis=1, concat_axis=0, tiled=True)
    by_column = jnp.moveaxis(blocked[:, 0], 1, 0)
    attend = functools.partial(
        lax.map,
        lambda column: column_update(column, key_bias, score_proj, value_gate, column_out),
    )
    left_part, right_part, gate_part = project_pair(pair_sum, pair_mask, triangle_in[0], width)
    left_part, right_part, by_column = lax.optimization_barrier(
        (left_part, right_part, by_column)
    )
    both = exchange_parts(left_part, right_part)
    half = rows_here // 2
    first = attend(by_column[:half])
    both, first = lax.optimization_barrier((both, first))
    share = width // devices
    products = jnp.einsum(
        "ick,jck->icj", both[:, :share], both[:, share:], preferred_element_type=jnp.float32
    ).astype(jnp.bfloat16)
    pair_sum = finish_triangle(pair_sum, return_products(products), gate_part, triangle_out[0])
    left_part, right_part, gate_part = project_pair(pair_sum, pair_mask, triangle_in[1], width)
    left_part, right_part, by_column = lax.optimization_barrier(
        (left_part, right_part, by_column)
    )
    both = exchange_parts(left_part, right_part)
    second = attend(by_column[half:])
    both, second = lax.optimization_barrier((both, second))
    products = jnp.einsum(
        "kci,kcj->icj", both[:, :share], both[:, share:], preferred_element_type=jnp.float32
    ).astype(jnp.bfloat16)
    attended = jnp.moveaxis(jnp.concatenate([first, second]), 0, 1)
    alignment_new = attended.reshape(attended.shape[0], rows_here, alignment.shape[2])
    pair_sum = finish_triangle(pair_sum, return_products(products), gate_part, triangle_out[1])
    return (alignment_new, pair_sum.astype(jnp.bfloat16))


def solution(mesh):
    placed = (
        P(("dp", "dap"), None, None),
        P(("dp", "dap"), None, None),
        P("dp"),
        P("dp"),
        P("dp"),
        P(),
        P(),
        P(),
        P(),
        P(),
        P(),
    )
    return jax.shard_map(
        on_device,
        mesh=mesh,
        in_specs=placed,
        out_specs=(P("dp", "dap", None), P(("dp", "dap"), None, None)),
        check_vma=False,
    )
```

```python
import functools

import jax
import jax.numpy as jnp
from jax import lax
from jax.experimental import pallas as pl
from jax.experimental.pallas import tpu as pltpu
from jax.sharding import PartitionSpec as P

HEADS = 8
HEAD_DIM = 32


EPS = 1e-05


def normalize(values, axis):
    average = jnp.mean(values, axis=axis, keepdims=True)
    centered = values - average
    variance = jnp.mean(centered * centered, axis=axis, keepdims=True)
    return centered * lax.rsqrt(variance + EPS)


def column_update(column, key_bias, score_proj, value_gate, column_out):
    count = column.shape[0]
    normed = normalize(column.astype(jnp.float32), 1).astype(jnp.bfloat16)
    queries = (
        jnp.dot(normed, score_proj[0], preferred_element_type=jnp.float32) * HEAD_DIM ** (-0.5)
    ).astype(jnp.bfloat16)
    key_rows = jnp.dot(normed, score_proj[1], preferred_element_type=jnp.float32).astype(
        jnp.bfloat16
    )
    value_rows = jnp.dot(normed, value_gate[0], preferred_element_type=jnp.float32).astype(
        jnp.bfloat16
    )
    gate_rows = jax.nn.sigmoid(jnp.dot(normed, value_gate[1], preferred_element_type=jnp.float32))
    queries = queries.reshape(count, HEADS, HEAD_DIM)
    key_rows = key_rows.reshape(count, HEADS, HEAD_DIM)
    value_rows = value_rows.reshape(count, HEADS, HEAD_DIM)
    scores = (
        jnp.einsum("shd,thd->hst", queries, key_rows, preferred_element_type=jnp.float32)
        + key_bias[None, None, :]
    )
    highest = jnp.max(scores, axis=-1, keepdims=True)
    raised = jnp.exp(scores - highest)
    weights = (raised / jnp.sum(raised, axis=-1, keepdims=True)).astype(jnp.bfloat16)
    mixture = jnp.einsum(
        "hst,thd->shd", weights, value_rows, preferred_element_type=jnp.float32
    ).reshape(count, HEADS * HEAD_DIM)
    gated = (gate_rows * mixture).astype(jnp.bfloat16)
    return (
        column.astype(jnp.float32) + jnp.dot(gated, column_out, preferred_element_type=jnp.float32)
    ).astype(jnp.bfloat16)


LANES = 128


def tiled(shape):
    return (shape[1] // LANES, shape[0], LANES)


def collect(staged, parts):
    for tile in range(staged.shape[0]):
        parts[:, tile * LANES : (tile + 1) * LANES] = staged[tile].astype(parts.dtype)


def scale_rows(values):
    average = jnp.mean(values, axis=0, keepdims=True)
    centered = values - average
    variance = jnp.mean(centered * centered, axis=0, keepdims=True)
    return (centered * lax.rsqrt(variance + EPS)).astype(jnp.bfloat16)


def project_row(row, pair_sum, pair_mask, weights, staged):
    sides = 2 * pair_sum.shape[0]
    rows = staged.shape[1] // sides
    projected = jnp.dot(weights, scale_rows(pair_sum), preferred_element_type=jnp.float32)
    parts = jax.nn.sigmoid(projected[:sides]) * projected[sides : 2 * sides] * pair_mask
    for tile in range(staged.shape[0]):
        staged[tile, pl.ds(row, sides, stride=rows), :] = parts[:, tile * LANES : (tile + 1) * LANES]
    return jax.nn.sigmoid(projected[2 * sides :])


def open_kernel(pair_act, same_chain, pair_mask, embed, weights, parts, pair_sum, gate, staged):
    for row in range(pair_act.shape[0]):
        channels = pair_act[row].astype(jnp.float32).T
        channels += jnp.where(same_chain[row : row + 1, :] > 0, embed[:, 0:1], embed[:, 1:2])
        pair_sum[row] = channels
        gate[row] = project_row(
            row, channels, pair_mask[row : row + 1, :], weights[...], staged
        )
    collect(staged, parts)


def update_row(row, pair_sum, products, gate, weights):
    rows = pair_sum.shape[0]
    width = products.shape[1] // rows
    tiles = [products[tile, pl.ds(row, width, stride=rows), :] for tile in range(products.shape[0])]
    normed = scale_rows(jnp.concatenate(tiles, axis=1))
    update = jnp.dot(weights, normed, preferred_element_type=jnp.float32)
    return pair_sum[row] + gate[row] * update


def middle_kernel(
    products, pair_sum, gate, pair_mask, weights_out, weights, parts, pair_next, gate_next, wide, staged
):
    for tile in range(wide.shape[0]):
        wide[tile] = products[:, tile * LANES : (tile + 1) * LANES].astype(jnp.float32)
    for row in range(pair_sum.shape[0]):
        channels = update_row(row, pair_sum, wide, gate, weights_out[...])
        pair_next[row] = channels
        gate_next[row] = project_row(
            row, channels, pair_mask[row : row + 1, :], weights[...], staged
        )
    collect(staged, parts)


def close_kernel(products, pair_sum, gate, weights_out, pair_new, wide):
    for tile in range(wide.shape[0]):
        wide[tile] = products[:, tile * LANES : (tile + 1) * LANES].astype(jnp.float32)
    for row in range(pair_sum.shape[0]):
        channels = update_row(row, pair_sum, wide, gate, weights_out[...])
        pair_new[row] = channels.T.astype(pair_new.dtype)


KERNEL = pltpu.CompilerParams(vmem_limit_bytes=40 * 1024 * 1024)


def open_pair(pair_act, same_chain, pair_mask, embed, weights):
    rows, side, channels = pair_act.shape
    flat = (2 * channels * rows, side)
    wide = jax.ShapeDtypeStruct((rows, channels, side), jnp.float32)
    return pl.pallas_call(
        open_kernel,
        out_shape=(jax.ShapeDtypeStruct(flat, jnp.bfloat16), wide, wide),
        scratch_shapes=[pltpu.VMEM(tiled(flat), jnp.float32)],
        compiler_params=KERNEL,
    )(pair_act, same_chain, pair_mask, embed, weights)


def middle_pair(products, pair_sum, gate, pair_mask, weights_out, weights):
    rows, channels, side = pair_sum.shape
    flat = (2 * channels * rows, side)
    wide = jax.ShapeDtypeStruct((rows, channels, side), jnp.float32)
    return pl.pallas_call(
        middle_kernel,
        out_shape=(jax.ShapeDtypeStruct(flat, jnp.bfloat16), wide, wide),
        scratch_shapes=[pltpu.VMEM(tiled(products.shape), jnp.float32), pltpu.VMEM(tiled(flat), jnp.float32)],
        compiler_params=KERNEL,
    )(products, pair_sum, gate, pair_mask, weights_out, weights)


def close_pair(products, pair_sum, gate, weights_out):
    rows, channels, side = pair_sum.shape
    return pl.pallas_call(
        close_kernel,
        out_shape=jax.ShapeDtypeStruct((rows, side, channels), jnp.bfloat16),
        scratch_shapes=[pltpu.VMEM(tiled(products.shape), jnp.float32)],
        compiler_params=KERNEL,
    )(products, pair_sum, gate, weights_out)


def order_weights(weights_in, width, devices):
    share = width // devices
    depth = weights_in.shape[0]
    groups = [
        weights_in[:, step * width : (step + 1) * width].T.reshape(devices, share, depth)
        for step in range(4)
    ]
    gates = jnp.concatenate([groups[0], groups[2]], axis=1).reshape(2 * width, depth)
    values = jnp.concatenate([groups[1], groups[3]], axis=1).reshape(2 * width, depth)
    return jnp.concatenate([gates, values, weights_in[:, 4 * width :].T])


def exchange(flat, devices):
    blocks = flat.reshape(devices, flat.shape[0] // devices, flat.shape[1])
    return lax.all_to_all(blocks, "dap", split_axis=0, concat_axis=0, tiled=True)


def split_parts(both, share, rows):
    devices, held, side = both.shape
    both = both.reshape(devices, 2, share, rows, side)
    return both[:, 0], both[:, 1]


def return_products(products, devices):
    share, side, _ = products.shape
    blocks = products.reshape(share, devices, side // devices, side)
    blocks = jnp.moveaxis(blocks, 0, 1).reshape(devices, -1, side)
    got = lax.all_to_all(blocks, "dap", split_axis=0, concat_axis=0, tiled=True)
    return got.reshape(-1, side)


def on_device(
    alignment,
    pair_act,
    crop_mask,
    seq_mask,
    chain_ids,
    chain_embed,
    score_proj,
    value_gate,
    column_out,
    triangle_in,
    triangle_out,
):
    rows_here = pair_act.shape[0]
    width = triangle_out.shape[1]
    devices = lax.axis_size("dap")
    row_start = lax.axis_index("dap") * rows_here
    share = width // devices
    seq_here = alignment.shape[0]
    blocked = alignment.reshape(seq_here, devices, rows_here, alignment.shape[2])
    blocked = lax.all_to_all(blocked, "dap", split_axis=1, concat_axis=0, tiled=True)
    by_column = jnp.moveaxis(blocked[:, 0], 1, 0)

    kept_rows = jnp.maximum(seq_mask, (jnp.arange(seq_mask.shape[0]) == 0).astype(jnp.int32))
    key_bias = (kept_rows - 1).astype(jnp.float32) * 1000000000.0
    crop = crop_mask.astype(jnp.float32)
    crop_rows = lax.dynamic_slice_in_dim(crop, row_start, rows_here)
    pair_mask = crop_rows[:, None] * crop[None, :]
    chain_rows = lax.dynamic_slice_in_dim(chain_ids, row_start, rows_here)
    same_chain = (chain_rows[:, None] == chain_ids[None, :]).astype(jnp.float32)
    ordered = [order_weights(triangle_in[step], width, devices) for step in range(2)]
    turned = [triangle_out[step].T for step in range(2)]

    attend = functools.partial(
        lax.map,
        lambda column: column_update(column, key_bias, score_proj, value_gate, column_out),
    )
    parts, pair_sum, gate = open_pair(
        pair_act, same_chain, pair_mask, chain_embed.T, ordered[0]
    )
    parts, blocked = lax.optimization_barrier((parts, blocked))
    by_column = jnp.moveaxis(blocked[:, 0], 1, 0)
    both = exchange(parts, devices)
    half = rows_here // 2
    first = attend(by_column[:half])
    both, first = lax.optimization_barrier((both, first))
    left, right = split_parts(both, share, rows_here)
    left = jnp.moveaxis(left, 1, 0).reshape(share, -1, left.shape[-1])
    right = jnp.moveaxis(right, 1, 0).reshape(share, -1, right.shape[-1])
    products = jnp.einsum(
        "cik,cjk->cij", left, right, preferred_element_type=jnp.float32
    ).astype(jnp.bfloat16)
    products = return_products(products, devices)
    parts, pair_sum, gate = middle_pair(
        products, pair_sum, gate, pair_mask, turned[0], ordered[1]
    )
    parts, blocked = lax.optimization_barrier((parts, blocked))
    by_column = jnp.moveaxis(blocked[:, 0], 1, 0)
    both = exchange(parts, devices)
    second = attend(by_column[half:])
    both, second = lax.optimization_barrier((both, second))
    left, right = split_parts(both, share, rows_here)
    left = jnp.moveaxis(left, 1, 0).reshape(share, -1, left.shape[-1])
    right = jnp.moveaxis(right, 1, 0).reshape(share, -1, right.shape[-1])
    products = jnp.einsum(
        "cki,ckj->cij", left, right, preferred_element_type=jnp.float32
    ).astype(jnp.bfloat16)
    products = return_products(products, devices)
    attended = jnp.moveaxis(jnp.concatenate([first, second]), 0, 1)
    alignment_new = attended.reshape(attended.shape[0], rows_here, alignment.shape[2])
    pair_new = close_pair(products, pair_sum, gate, turned[1])
    return (alignment_new, pair_new)


def solution(mesh):
    placed = (
        P(("dp", "dap"), None, None),
        P(("dp", "dap"), None, None),
        P("dp"),
        P("dp"),
        P("dp"),
        P(),
        P(),
        P(),
        P(),
        P(),
        P(),
    )
    return jax.shard_map(
        on_device,
        mesh=mesh,
        in_specs=placed,
        out_specs=(P("dp", "dap", None), P(("dp", "dap"), None, None)),
        check_vma=False,
    )
```

```python
import jax
import jax.numpy as jnp
from jax import lax
from jax.experimental import pallas as pl
from jax.experimental.pallas import tpu as pltpu
from jax.sharding import PartitionSpec as P

HEADS = 8
HEAD_DIM = 32


EPS = 1e-05


def normalize(values, axis):
    average = jnp.mean(values, axis=axis, keepdims=True)
    centered = values - average
    variance = jnp.mean(centered * centered, axis=axis, keepdims=True)
    return centered * lax.rsqrt(variance + EPS)


LANES = 128


def collect(staged, parts):
    sides, tiles, _, lanes = staged.shape
    held = parts.shape[1] // sides
    for side in range(sides):
        for tile in range(tiles):
            piece = staged[side, tile].reshape(parts.shape[0], held, lanes)
            parts[:, side * held : (side + 1) * held, tile * lanes : (tile + 1) * lanes] = (
                piece.astype(parts.dtype)
            )


def scale_rows(values):
    average = jnp.mean(values, axis=0, keepdims=True)
    centered = values - average
    variance = jnp.mean(centered * centered, axis=0, keepdims=True)
    return (centered * lax.rsqrt(variance + EPS)).astype(jnp.bfloat16)


def turn(values):
    return values.astype(jnp.float32).T.astype(values.dtype)


def project(normed, weights):
    return jnp.dot(weights, normed, preferred_element_type=jnp.float32)


def stage_row(row, rows, channels, weights, mask, staged):
    projected = project(scale_rows(channels), weights)
    width = staged.shape[2] // rows
    for side in range(2):
        gates, values = (
            projected[step * width : (step + 1) * width] for step in (2 * side, 2 * side + 1)
        )
        parts = jax.nn.sigmoid(gates) * values * mask
        for tile in range(staged.shape[1]):
            staged[side, tile, pl.ds(row, width, stride=rows), :] = parts[
                :, tile * LANES : (tile + 1) * LANES
            ]


def widen(products, wide):
    devices, held, lanes = products.shape
    held = held * lanes // (wide.shape[0] * LANES)
    for tile in range(wide.shape[0]):
        half, lane = divmod(tile * LANES, lanes)
        piece = products[:, half * held : (half + 1) * held, lane : lane + LANES]
        wide[tile] = piece.astype(jnp.float32).reshape(wide.shape[1:])


def update_row(row, rows, wide, weights_out):
    width = wide.shape[1] // rows
    tiles = [wide[tile, pl.ds(row, width, stride=rows), :] for tile in range(wide.shape[0])]
    return project(scale_rows(jnp.concatenate(tiles, axis=1)), weights_out)


def open_row(row, place, chain_each, chain_all, embed, pair_act):
    same_embed, other_embed = (
        jnp.broadcast_to(embed[step : step + 1, :], (8, embed.shape[1])).T[:, 0:1]
        for step in range(2)
    )
    same = chain_all[...] == chain_each[place]
    return pair_act[row].astype(jnp.float32).T + jnp.where(same, same_embed, other_embed)


def open_kernel(
    first, crop_each, chain_each, crop_all, chain_all, embed, weights_in, pair_act, parts, staged
):
    rows = pair_act.shape[0]
    width = staged.shape[2] // rows
    weights = turn(weights_in[0][:, : 4 * width])
    crop = crop_all[...].astype(jnp.float32)
    for row in range(rows):
        place = first[0] + row
        channels = open_row(row, place, chain_each, chain_all, embed, pair_act)
        mask = crop * crop_each[place].astype(jnp.float32)
        stage_row(row, rows, channels, weights, mask, staged)
    collect(staged, parts)


def gate_of(channels, weights):
    return jax.nn.sigmoid(project(scale_rows(channels), weights))


def open_gate_kernel(first, chain_each, chain_all, embed, weights_in, pair_act, pair_sum, gate):
    weights = turn(weights_in[0][:, weights_in.shape[2] - pair_sum.shape[1] :])
    for row in range(pair_act.shape[0]):
        channels = open_row(row, first[0] + row, chain_each, chain_all, embed, pair_act)
        pair_sum[row] = channels
        gate[row] = gate_of(channels, weights)


def start_copies(source, target, sems, row):
    copies = [
        pltpu.make_async_copy(one.at[row], other.at[row], sems.at[side, row])
        for side, (one, other) in enumerate(zip(source, target))
    ]
    for copy in copies:
        copy.start()
    return copies


def middle_kernel(
    first,
    crop_each,
    crop_all,
    weights_out,
    weights_in,
    products,
    pair_from,
    gate_from,
    parts,
    pair_far,
    wide,
    staged,
    pair_sum,
    gate,
    pair_next,
    sems,
    next_sems,
):
    rows = pair_sum.shape[0]
    width = staged.shape[2] // rows
    arriving = [
        start_copies((pair_from, gate_from), (pair_sum, gate), sems, row) for row in range(rows)
    ]
    widen(products, wide)
    weights, turned = turn(weights_in[1][:, : 4 * width]), turn(weights_out[0])
    crop = crop_all[...].astype(jnp.float32)
    leaving = []
    for row in range(rows):
        mask = crop * crop_each[first[0] + row].astype(jnp.float32)
        update = update_row(row, rows, wide, turned)
        for copy in arriving[row]:
            copy.wait()
        channels = pair_sum[row] + gate[row] * update
        pair_next[row] = channels
        leaving += start_copies((pair_next,), (pair_far,), next_sems, row)
        stage_row(row, rows, channels, weights, mask, staged)
    collect(staged, parts)
    for copy in leaving:
        copy.wait()


def middle_gate_kernel(weights_in, pair_sum, gate):
    weights = turn(weights_in[1][:, weights_in.shape[2] - pair_sum.shape[1] :])
    for row in range(pair_sum.shape[0]):
        gate[row] = gate_of(pair_sum[row], weights)


def close_kernel(
    weights_out, products, pair_from, gate_from, pair_new, wide, pair_sum, gate, sems
):
    rows = pair_sum.shape[0]
    arriving = [
        start_copies((pair_from, gate_from), (pair_sum, gate), sems, row) for row in range(rows)
    ]
    widen(products, wide)
    turned = turn(weights_out[1])
    for row in range(rows):
        update = update_row(row, rows, wide, turned)
        for copy in arriving[row]:
            copy.wait()
        pair_new[row] = (pair_sum[row] + gate[row] * update).T.astype(pair_new.dtype)


def attend_kernel(key_bias, score_proj, value_gate, column_out, got, out, wide, staged):
    tiles, held, _ = wide.shape
    seqs = key_bias.shape[0]
    rows = held // seqs
    for tile in range(tiles):
        piece = got[:, :, tile * LANES : (tile + 1) * LANES]
        wide[tile] = piece.astype(jnp.float32).reshape(held, LANES)
    query, value, gates, last = (
        turn(weights) for weights in (score_proj[0], value_gate[0], value_gate[1], column_out[...])
    )
    bias = jnp.broadcast_to(key_bias[...], (seqs, seqs))

    def attend(row, carry):
        column = jnp.concatenate(
            [wide[tile, pl.ds(row, seqs, stride=rows), :] for tile in range(tiles)], axis=1
        )
        normed_wide = normalize(column, 1)
        normed = normed_wide.astype(jnp.bfloat16)
        turned = normed_wide.T.astype(jnp.bfloat16)
        queries = (project(turned, query) * HEAD_DIM ** (-0.5)).astype(jnp.bfloat16)
        key_rows = project(score_proj[1], normed).astype(jnp.bfloat16)
        value_rows = project(turned, value).astype(jnp.bfloat16)
        gate_rows = jax.nn.sigmoid(project(turned, gates))
        mixture = []
        for head in range(HEADS):
            span = slice(head * HEAD_DIM, (head + 1) * HEAD_DIM)
            scores = project(queries[span], key_rows[:, span]) + bias
            raised = jnp.exp(scores - jnp.max(scores, axis=0, keepdims=True))
            weights = raised * (1.0 / jnp.sum(raised, axis=0, keepdims=True))
            mixture.append(project(weights.astype(jnp.bfloat16), value_rows[span]))
        gated = (gate_rows * jnp.concatenate(mixture, axis=0)).astype(jnp.bfloat16)
        column += project(gated, last).T
        for tile in range(tiles):
            staged[tile, pl.ds(row, seqs, stride=rows), :] = column[
                :, tile * LANES : (tile + 1) * LANES
            ]
        return carry

    lax.fori_loop(0, rows, attend, 0)
    for tile in range(tiles):
        out[:, tile * LANES : (tile + 1) * LANES] = staged[tile].astype(out.dtype)


KERNEL = pltpu.CompilerParams(vmem_limit_bytes=60 * 1024 * 1024)
HERE = pl.BlockSpec(memory_space=pltpu.VMEM)
EACH = pl.BlockSpec(memory_space=pltpu.SMEM)
FAR = pl.BlockSpec(memory_space=pl.ANY)


def shapes_of(rows, side, channels, devices):
    parts = jax.ShapeDtypeStruct((devices, 2 * channels * rows // devices, side), jnp.bfloat16)
    held = jax.ShapeDtypeStruct((rows, channels, side), jnp.float32)
    tiles = (side // LANES, channels * rows, LANES)
    return (
        parts,
        held,
        pltpu.VMEM(tiles, jnp.float32),
        pltpu.VMEM((2,) + tiles, jnp.float32),
    )


def open_pair(first, crop, chains, embed, weights_in, pair_act, devices):
    parts, _, _, staged = shapes_of(*pair_act.shape, devices)
    return pl.pallas_call(
        open_kernel,
        in_specs=[EACH] * 3 + [HERE] * 5,
        out_specs=HERE,
        out_shape=parts,
        scratch_shapes=[staged],
        compiler_params=KERNEL,
    )(first, crop, chains, crop[None], chains[None], embed, weights_in, pair_act)


def open_gate(first, chains, embed, weights_in, pair_act, devices):
    _, held, _, _ = shapes_of(*pair_act.shape, devices)
    return pl.pallas_call(
        open_gate_kernel,
        in_specs=[EACH] * 2 + [HERE] * 4,
        out_specs=(HERE, HERE),
        out_shape=(held, held),
        compiler_params=KERNEL,
    )(first, chains, chains[None], embed, weights_in, pair_act)


def middle_pair(first, crop, weights_out, weights_in, products, pair_sum, gate):
    rows, channels, side = pair_sum.shape
    devices, held, lanes = products.shape
    parts, pair_next, wide, staged = shapes_of(rows, side, channels, devices)
    near = pltpu.VMEM(pair_sum.shape, jnp.float32)
    return pl.pallas_call(
        middle_kernel,
        grid=(1,),
        in_specs=[EACH] * 2
        + [HERE] * 3
        + [pl.BlockSpec((devices, held // 2, lanes), lambda step: (0, 0, 0)), FAR, FAR],
        out_specs=(HERE, FAR),
        out_shape=(parts, pair_next),
        scratch_shapes=[wide, staged, near, near, near]
        + [pltpu.SemaphoreType.DMA((2, rows)), pltpu.SemaphoreType.DMA((1, rows))],
        compiler_params=KERNEL,
    )(first, crop, crop[None], weights_out, weights_in, products, pair_sum, gate)


def middle_gate(weights_in, pair_sum):
    return pl.pallas_call(
        middle_gate_kernel,
        in_specs=[HERE] * 2,
        out_specs=HERE,
        out_shape=jax.ShapeDtypeStruct(pair_sum.shape, jnp.float32),
        compiler_params=KERNEL,
    )(weights_in, pair_sum)


def close_pair(weights_out, products, pair_sum, gate):
    rows, channels, side = pair_sum.shape
    _, _, wide, _ = shapes_of(rows, side, channels, products.shape[0])
    near = pltpu.VMEM(pair_sum.shape, jnp.float32)
    return pl.pallas_call(
        close_kernel,
        in_specs=[HERE] * 2 + [FAR] * 2,
        out_specs=HERE,
        out_shape=jax.ShapeDtypeStruct((rows, side, channels), jnp.bfloat16),
        scratch_shapes=[wide, near, near, pltpu.SemaphoreType.DMA((2, rows))],
        compiler_params=KERNEL,
    )(weights_out, products, pair_sum, gate)


def attend_columns(key_bias, score_proj, value_gate, column_out, got, rows):
    devices, held, depth = got.shape
    seqs = key_bias.shape[0]
    wide = pltpu.VMEM((depth // LANES, seqs * rows, LANES), jnp.float32)
    moves = seqs * depth * (4 * depth + 2 * seqs + depth)
    return pl.pallas_call(
        attend_kernel,
        grid=(1,),
        in_specs=[HERE] * 4 + [pl.BlockSpec((devices, held // 2, depth), lambda step: (0, 1, 0))],
        out_specs=HERE,
        out_shape=jax.ShapeDtypeStruct((seqs * rows, depth), jnp.bfloat16),
        scratch_shapes=[wide, wide],
        compiler_params=KERNEL,
        cost_estimate=pl.CostEstimate(
            flops=2 * rows * moves,
            bytes_accessed=4 * seqs * rows * depth,
            transcendentals=rows * seqs * (HEADS * seqs + depth),
        ),
    )(key_bias[:, None], score_proj, value_gate, column_out, got)


def split_parts(both, share, rows):
    devices, held, side = both.shape
    both = both.reshape(devices, 2, share, rows, side)
    return both[:, 0], both[:, 1]


def block_products(products, devices, lanes):
    share, side, _ = products.shape
    blocks = products.reshape(share, devices, side // devices, side // lanes, lanes)
    return blocks.transpose(1, 3, 0, 2, 4).reshape(devices, -1, lanes)


def exchange_blocks(blocks):
    return lax.all_to_all(blocks, "dap", split_axis=0, concat_axis=0, tiled=True)


def on_device(
    alignment,
    pair_act,
    crop_mask,
    seq_mask,
    chain_ids,
    chain_embed,
    score_proj,
    value_gate,
    column_out,
    triangle_in,
    triangle_out,
):
    rows_here = pair_act.shape[0]
    width = triangle_out.shape[1]
    devices = lax.axis_size("dap")
    row_start = lax.axis_index("dap") * rows_here
    share = width // devices
    seq_here, _, depth = alignment.shape
    sent = alignment.reshape(seq_here, devices, rows_here, depth)
    sent = jnp.moveaxis(sent, 1, 0).reshape(devices, -1, depth)
    carrier = jnp.concatenate([jnp.zeros_like(sent), sent], axis=1)

    kept_rows = jnp.maximum(seq_mask, (jnp.arange(seq_mask.shape[0]) == 0).astype(jnp.int32))
    key_bias = (kept_rows - 1).astype(jnp.float32) * 1000000000.0
    first_row = row_start.reshape(1).astype(jnp.int32)
    parts = open_pair(
        first_row, crop_mask, chain_ids, chain_embed, triangle_in, pair_act, devices
    )
    both = exchange_blocks(parts)
    pair_sum, gate = open_gate(first_row, chain_ids, chain_embed, triangle_in, pair_act, devices)
    both, carrier, pair_sum, gate = lax.optimization_barrier((both, carrier, pair_sum, gate))
    left, right = split_parts(both, share, rows_here)
    left = jnp.moveaxis(left, 1, 0).reshape(share, -1, left.shape[-1])
    right = jnp.moveaxis(right, 1, 0).reshape(share, -1, right.shape[-1])
    products = jnp.einsum(
        "cik,cjk->cij", left, right, preferred_element_type=jnp.float32
    ).astype(jnp.bfloat16)
    products = block_products(products, devices, depth)
    got = exchange_blocks(lax.dynamic_update_slice(carrier, products, (0, 0, 0)))
    parts, pair_sum = middle_pair(
        first_row, crop_mask, triangle_out, triangle_in, got, pair_sum, gate
    )
    parts, got = lax.optimization_barrier((parts, got))
    both = exchange_blocks(parts)
    attended = attend_columns(key_bias, score_proj, value_gate, column_out, got, rows_here)
    both, attended, pair_sum = lax.optimization_barrier((both, attended, pair_sum))
    left, right = split_parts(both, share, rows_here)
    left = jnp.moveaxis(left, 1, 0).reshape(share, -1, left.shape[-1])
    right = jnp.moveaxis(right, 1, 0).reshape(share, -1, right.shape[-1])
    products = jnp.einsum(
        "cki,ckj->cij", left, right, preferred_element_type=jnp.float32
    ).astype(jnp.bfloat16)
    products = exchange_blocks(block_products(products, devices, products.shape[-1]))
    gate = middle_gate(triangle_in, pair_sum)
    alignment_new = attended.reshape(-1, rows_here, depth)
    products, gate = lax.optimization_barrier((products, gate))
    pair_new = close_pair(triangle_out, products, pair_sum, gate)
    return (alignment_new, pair_new)


def solution(mesh):
    placed = (
        P(("dp", "dap"), None, None),
        P(("dp", "dap"), None, None),
        P("dp"),
        P("dp"),
        P("dp"),
        P(),
        P(),
        P(),
        P(),
        P(),
        P(),
    )
    return jax.shard_map(
        on_device,
        mesh=mesh,
        in_specs=placed,
        out_specs=(P("dp", "dap", None), P(("dp", "dap"), None, None)),
        check_vma=False,
    )
```

```python
import jax
import jax.numpy as jnp
from jax import lax
from jax.experimental import pallas as pl
from jax.experimental.pallas import tpu as pltpu
from jax.sharding import PartitionSpec as P

HEADS = 8
HEAD_DIM = 32


EPS = 1e-05


def normalize(values, axis):
    average = jnp.mean(values, axis=axis, keepdims=True)
    centered = values - average
    variance = jnp.mean(centered * centered, axis=axis, keepdims=True)
    return centered * lax.rsqrt(variance + EPS)


LANES = 128


def collect(staged, parts):
    sides, tiles, _, lanes = staged.shape
    held = parts.shape[1] // sides
    for side in range(sides):
        for tile in range(tiles):
            piece = staged[side, tile].reshape(parts.shape[0], held, lanes)
            parts[:, side * held : (side + 1) * held, tile * lanes : (tile + 1) * lanes] = (
                piece.astype(parts.dtype)
            )


def scale_rows(values):
    average = jnp.mean(values, axis=0, keepdims=True)
    centered = values - average
    variance = jnp.mean(centered * centered, axis=0, keepdims=True)
    return (centered * lax.rsqrt(variance + EPS)).astype(jnp.bfloat16)


def turn(values):
    return values.astype(jnp.float32).T.astype(values.dtype)


def project(normed, weights):
    return jnp.dot(weights, normed, preferred_element_type=jnp.float32)


def stage_row(row, rows, channels, weights, mask, staged):
    projected = project(scale_rows(channels), weights)
    width = staged.shape[2] // rows
    for side in range(2):
        gates, values = (
            projected[step * width : (step + 1) * width] for step in (2 * side, 2 * side + 1)
        )
        parts = jax.nn.sigmoid(gates) * values * mask
        for tile in range(staged.shape[1]):
            staged[side, tile, pl.ds(row, width, stride=rows), :] = parts[
                :, tile * LANES : (tile + 1) * LANES
            ]


def widen(products, wide):
    devices, held, lanes = products.shape
    held = held * lanes // (wide.shape[0] * LANES)
    for tile in range(wide.shape[0]):
        half, lane = divmod(tile * LANES, lanes)
        piece = products[:, half * held : (half + 1) * held, lane : lane + LANES]
        wide[tile] = piece.astype(jnp.float32).reshape(wide.shape[1:])


def update_row(row, rows, wide, weights_out):
    width = wide.shape[1] // rows
    tiles = [wide[tile, pl.ds(row, width, stride=rows), :] for tile in range(wide.shape[0])]
    return project(scale_rows(jnp.concatenate(tiles, axis=1)), weights_out)


def open_row(row, place, chain_each, chain_all, embed, pair_act):
    same_embed, other_embed = (
        jnp.broadcast_to(embed[step : step + 1, :], (8, embed.shape[1])).T[:, 0:1]
        for step in range(2)
    )
    same = chain_all[...] == chain_each[place]
    return pair_act[row].astype(jnp.float32).T + jnp.where(same, same_embed, other_embed)


def open_kernel(
    first, crop_each, chain_each, crop_all, chain_all, embed, weights_in, pair_act, parts, staged
):
    rows = pair_act.shape[0]
    width = staged.shape[2] // rows
    weights = turn(weights_in[0][:, : 4 * width])
    crop = crop_all[...].astype(jnp.float32)
    for row in range(rows):
        place = first[0] + row
        channels = open_row(row, place, chain_each, chain_all, embed, pair_act)
        mask = crop * crop_each[place].astype(jnp.float32)
        stage_row(row, rows, channels, weights, mask, staged)
    collect(staged, parts)


def gate_of(channels, weights):
    return jax.nn.sigmoid(project(scale_rows(channels), weights))


def open_gate_kernel(first, chain_each, chain_all, embed, weights_in, pair_act, gate):
    weights = turn(weights_in[0][:, weights_in.shape[2] - gate.shape[1] :])
    for row in range(pair_act.shape[0]):
        channels = open_row(row, first[0] + row, chain_each, chain_all, embed, pair_act)
        gate[row] = gate_of(channels, weights).astype(gate.dtype)


def start_copies(source, target, sems, row):
    copies = [
        pltpu.make_async_copy(one.at[row], other.at[row], sems.at[side, row])
        for side, (one, other) in enumerate(zip(source, target))
    ]
    for copy in copies:
        copy.start()
    return copies


def middle_kernel(
    first,
    crop_each,
    chain_each,
    crop_all,
    chain_all,
    embed,
    weights_out,
    weights_in,
    products,
    pair_from,
    gate_from,
    parts,
    wide,
    staged,
    pair_act,
    gate,
    updates,
    sems,
):
    rows = pair_act.shape[0]
    width = staged.shape[2] // rows
    arriving = [
        start_copies((pair_from, gate_from), (pair_act, gate), sems, row) for row in range(rows)
    ]
    widen(products, wide)
    weights, turned = turn(weights_in[1][:, : 4 * width]), turn(weights_out[0])
    crop = crop_all[...].astype(jnp.float32)
    for row in range(rows):
        updates[row] = update_row(row, rows, wide, turned)
    for copies in arriving:
        for copy in copies:
            copy.wait()
    for row in range(rows):
        place = first[0] + row
        mask = crop * crop_each[place].astype(jnp.float32)
        channels = open_row(row, place, chain_each, chain_all, embed, pair_act)
        channels += gate[row].astype(jnp.float32) * updates[row]
        stage_row(row, rows, channels, weights, mask, staged)
    collect(staged, parts)


def middle_gate_kernel(
    first,
    chain_each,
    chain_all,
    embed,
    weights_out,
    weights_in,
    products,
    pair_act,
    gate,
    pair_next,
    gate_next,
    wide,
):
    rows = pair_act.shape[0]
    weights = turn(weights_in[1][:, weights_in.shape[2] - gate.shape[1] :])
    widen(products, wide)
    turned = turn(weights_out[0])
    for row in range(rows):
        channels = open_row(row, first[0] + row, chain_each, chain_all, embed, pair_act)
        channels += gate[row].astype(jnp.float32) * update_row(row, rows, wide, turned)
        pair_next[row] = channels
        gate_next[row] = gate_of(channels, weights).astype(gate_next.dtype)


def close_kernel(
    weights_out, products, pair_from, gate_from, pair_new, wide, pair_sum, gate, updates, sems
):
    rows = pair_sum.shape[0]
    arriving = [
        start_copies((pair_from, gate_from), (pair_sum, gate), sems, row) for row in range(rows)
    ]
    widen(products, wide)
    turned = turn(weights_out[1])
    for row in range(rows):
        updates[row] = update_row(row, rows, wide, turned)
    for copies in arriving:
        for copy in copies:
            copy.wait()
    for row in range(rows):
        channels = pair_sum[row] + gate[row].astype(jnp.float32) * updates[row]
        pair_new[row] = channels.T.astype(pair_new.dtype)


def attend_kernel(key_bias, score_proj, value_gate, column_out, got, out, wide, staged):
    tiles, held, _ = wide.shape
    seqs = key_bias.shape[0]
    rows = held // seqs
    for tile in range(tiles):
        piece = got[:, :, tile * LANES : (tile + 1) * LANES]
        wide[tile] = piece.astype(jnp.float32).reshape(held, LANES)
    query, value, gates, last = (
        turn(weights) for weights in (score_proj[0], value_gate[0], value_gate[1], column_out[...])
    )
    bias = jnp.broadcast_to(key_bias[...], (seqs, seqs))

    def attend(row, carry):
        column = jnp.concatenate(
            [wide[tile, pl.ds(row, seqs, stride=rows), :] for tile in range(tiles)], axis=1
        )
        normed_wide = normalize(column, 1)
        normed = normed_wide.astype(jnp.bfloat16)
        turned = normed_wide.T.astype(jnp.bfloat16)
        queries = (project(turned, query) * HEAD_DIM ** (-0.5)).astype(jnp.bfloat16)
        key_rows = project(score_proj[1], normed).astype(jnp.bfloat16)
        value_rows = project(turned, value).astype(jnp.bfloat16)
        gate_rows = jax.nn.sigmoid(project(turned, gates))
        mixture = []
        for head in range(HEADS):
            span = slice(head * HEAD_DIM, (head + 1) * HEAD_DIM)
            scores = project(queries[span], key_rows[:, span]) + bias
            raised = jnp.exp(scores - jnp.max(scores, axis=0, keepdims=True))
            weights = raised * (1.0 / jnp.sum(raised, axis=0, keepdims=True))
            mixture.append(project(weights.astype(jnp.bfloat16), value_rows[span]))
        gated = (gate_rows * jnp.concatenate(mixture, axis=0)).astype(jnp.bfloat16)
        column += project(gated, last).T
        for tile in range(tiles):
            staged[tile, pl.ds(row, seqs, stride=rows), :] = column[
                :, tile * LANES : (tile + 1) * LANES
            ]
        return carry

    lax.fori_loop(0, rows, attend, 0)
    for tile in range(tiles):
        out[:, tile * LANES : (tile + 1) * LANES] = staged[tile].astype(out.dtype)


KERNEL = pltpu.CompilerParams(vmem_limit_bytes=60 * 1024 * 1024)
HERE = pl.BlockSpec(memory_space=pltpu.VMEM)
EACH = pl.BlockSpec(memory_space=pltpu.SMEM)
FAR = pl.BlockSpec(memory_space=pl.ANY)


def shapes_of(rows, side, channels, devices):
    parts = jax.ShapeDtypeStruct((devices, 2 * channels * rows // devices, side), jnp.bfloat16)
    held = jax.ShapeDtypeStruct((rows, channels, side), jnp.float32)
    tiles = (side // LANES, channels * rows, LANES)
    return (
        parts,
        held,
        pltpu.VMEM(tiles, jnp.float32),
        pltpu.VMEM((2,) + tiles, jnp.float32),
    )


def open_pair(first, crop, chains, embed, weights_in, pair_act, devices):
    parts, _, _, staged = shapes_of(*pair_act.shape, devices)
    return pl.pallas_call(
        open_kernel,
        in_specs=[EACH] * 3 + [HERE] * 5,
        out_specs=HERE,
        out_shape=parts,
        scratch_shapes=[staged],
        compiler_params=KERNEL,
    )(first, crop, chains, crop[None], chains[None], embed, weights_in, pair_act)


def open_gate(first, chains, embed, weights_in, pair_act):
    rows, side, channels = pair_act.shape
    return pl.pallas_call(
        open_gate_kernel,
        in_specs=[EACH] * 2 + [HERE] * 4,
        out_specs=HERE,
        out_shape=jax.ShapeDtypeStruct((rows, channels, side), jnp.bfloat16),
        compiler_params=KERNEL,
    )(first, chains, chains[None], embed, weights_in, pair_act)


def first_half(blocks):
    devices, held, lanes = blocks.shape
    return pl.BlockSpec((devices, held // 2, lanes), lambda step: (0, 0, 0))


def middle_pair(first, crop, chains, embed, weights_out, weights_in, products, pair_act, gate):
    parts, held, wide, staged = shapes_of(*pair_act.shape, products.shape[0])
    rows = pair_act.shape[0]
    return pl.pallas_call(
        middle_kernel,
        grid=(1,),
        in_specs=[EACH] * 3 + [HERE] * 5 + [first_half(products), FAR, FAR],
        out_specs=HERE,
        out_shape=parts,
        scratch_shapes=[
            wide,
            staged,
            pltpu.VMEM(pair_act.shape, pair_act.dtype),
            pltpu.VMEM(gate.shape, gate.dtype),
            pltpu.VMEM(held.shape, held.dtype),
            pltpu.SemaphoreType.DMA((2, rows)),
        ],
        compiler_params=KERNEL,
    )(
        first,
        crop,
        chains,
        crop[None],
        chains[None],
        embed,
        weights_out,
        weights_in,
        products,
        pair_act,
        gate,
    )


def middle_gate(first, chains, embed, weights_out, weights_in, products, pair_act, gate):
    _, held, wide, _ = shapes_of(*pair_act.shape, products.shape[0])
    return pl.pallas_call(
        middle_gate_kernel,
        grid=(1,),
        in_specs=[EACH] * 2 + [HERE] * 4 + [first_half(products), HERE, HERE],
        out_specs=(HERE, HERE),
        out_shape=(held, jax.ShapeDtypeStruct(gate.shape, gate.dtype)),
        scratch_shapes=[wide],
        compiler_params=KERNEL,
    )(first, chains, chains[None], embed, weights_out, weights_in, products, pair_act, gate)


def close_pair(weights_out, products, pair_sum, gate):
    rows, channels, side = pair_sum.shape
    _, _, wide, _ = shapes_of(rows, side, channels, products.shape[0])
    near = pltpu.VMEM(pair_sum.shape, jnp.float32)
    return pl.pallas_call(
        close_kernel,
        in_specs=[HERE] * 2 + [FAR] * 2,
        out_specs=HERE,
        out_shape=jax.ShapeDtypeStruct((rows, side, channels), jnp.bfloat16),
        scratch_shapes=[
            wide,
            near,
            pltpu.VMEM(gate.shape, gate.dtype),
            near,
            pltpu.SemaphoreType.DMA((2, rows)),
        ],
        compiler_params=KERNEL,
    )(weights_out, products, pair_sum, gate)


def attend_columns(key_bias, score_proj, value_gate, column_out, got, rows):
    devices, held, depth = got.shape
    seqs = key_bias.shape[0]
    wide = pltpu.VMEM((depth // LANES, seqs * rows, LANES), jnp.float32)
    moves = seqs * depth * (4 * depth + 2 * seqs + depth)
    return pl.pallas_call(
        attend_kernel,
        grid=(1,),
        in_specs=[HERE] * 4 + [pl.BlockSpec((devices, held // 2, depth), lambda step: (0, 1, 0))],
        out_specs=HERE,
        out_shape=jax.ShapeDtypeStruct((seqs * rows, depth), jnp.bfloat16),
        scratch_shapes=[wide, wide],
        compiler_params=KERNEL,
        cost_estimate=pl.CostEstimate(
            flops=2 * rows * moves,
            bytes_accessed=4 * seqs * rows * depth,
            transcendentals=rows * seqs * (HEADS * seqs + depth),
        ),
    )(key_bias[:, None], score_proj, value_gate, column_out, got)


def split_parts(both, share, rows):
    devices, held, side = both.shape
    both = both.reshape(devices, 2, share, rows, side)
    return both[:, 0], both[:, 1]


def block_products(products, devices, lanes):
    share, side, _ = products.shape
    blocks = products.reshape(share, devices, side // devices, side // lanes, lanes)
    return blocks.transpose(1, 3, 0, 2, 4).reshape(devices, -1, lanes)


def exchange_blocks(blocks):
    return lax.all_to_all(blocks, "dap", split_axis=0, concat_axis=0, tiled=True)


def on_device(
    alignment,
    pair_act,
    crop_mask,
    seq_mask,
    chain_ids,
    chain_embed,
    score_proj,
    value_gate,
    column_out,
    triangle_in,
    triangle_out,
):
    rows_here = pair_act.shape[0]
    width = triangle_out.shape[1]
    devices = lax.axis_size("dap")
    row_start = lax.axis_index("dap") * rows_here
    share = width // devices
    seq_here, _, depth = alignment.shape
    sent = alignment.reshape(seq_here, devices, rows_here, depth)
    sent = jnp.moveaxis(sent, 1, 0).reshape(devices, -1, depth)
    carrier = jnp.concatenate([jnp.zeros_like(sent), sent], axis=1)

    kept_rows = jnp.maximum(seq_mask, (jnp.arange(seq_mask.shape[0]) == 0).astype(jnp.int32))
    key_bias = (kept_rows - 1).astype(jnp.float32) * 1000000000.0
    first_row = row_start.reshape(1).astype(jnp.int32)
    parts = open_pair(
        first_row, crop_mask, chain_ids, chain_embed, triangle_in, pair_act, devices
    )
    both = exchange_blocks(parts)
    gate = open_gate(first_row, chain_ids, chain_embed, triangle_in, pair_act)
    both, carrier, gate = lax.optimization_barrier((both, carrier, gate))
    left, right = split_parts(both, share, rows_here)
    left = jnp.moveaxis(left, 1, 0).reshape(share, -1, left.shape[-1])
    right = jnp.moveaxis(right, 1, 0).reshape(share, -1, right.shape[-1])
    products = jnp.einsum(
        "cik,cjk->cij", left, right, preferred_element_type=jnp.float32
    ).astype(jnp.bfloat16)
    products = block_products(products, devices, depth)
    got = exchange_blocks(lax.dynamic_update_slice(carrier, products, (0, 0, 0)))
    pair_in = (chain_embed, triangle_out, triangle_in)
    parts = middle_pair(first_row, crop_mask, chain_ids, *pair_in, got, pair_act, gate)
    parts, got = lax.optimization_barrier((parts, got))
    both = exchange_blocks(parts)
    attended = attend_columns(key_bias, score_proj, value_gate, column_out, got, rows_here)
    both, attended, got = lax.optimization_barrier((both, attended, got))
    left, right = split_parts(both, share, rows_here)
    left = jnp.moveaxis(left, 1, 0).reshape(share, -1, left.shape[-1])
    right = jnp.moveaxis(right, 1, 0).reshape(share, -1, right.shape[-1])
    products = jnp.einsum(
        "cki,ckj->cij", left, right, preferred_element_type=jnp.float32
    ).astype(jnp.bfloat16)
    products = exchange_blocks(block_products(products, devices, products.shape[-1]))
    pair_sum, gate = middle_gate(first_row, chain_ids, *pair_in, got, pair_act, gate)
    alignment_new = attended.reshape(-1, rows_here, depth)
    products, pair_sum, gate = lax.optimization_barrier((products, pair_sum, gate))
    pair_new = close_pair(triangle_out, products, pair_sum, gate)
    return (alignment_new, pair_new)


def solution(mesh):
    placed = (
        P(("dp", "dap"), None, None),
        P(("dp", "dap"), None, None),
        P("dp"),
        P("dp"),
        P("dp"),
        P(),
        P(),
        P(),
        P(),
        P(),
        P(),
    )
    return jax.shard_map(
        on_device,
        mesh=mesh,
        in_specs=placed,
        out_specs=(P("dp", "dap", None), P(("dp", "dap"), None, None)),
        check_vma=False,
    )
```

```python
import jax
import jax.numpy as jnp
from jax import lax
from jax.experimental import pallas as pl
from jax.experimental.pallas import tpu as pltpu
from jax.sharding import PartitionSpec as P

HEADS = 8
HEAD_DIM = 32


EPS = 1e-05


def normalize(values, axis):
    average = jnp.mean(values, axis=axis, keepdims=True)
    centered = values - average
    variance = jnp.mean(centered * centered, axis=axis, keepdims=True)
    return centered * lax.rsqrt(variance + EPS)


LANES = 128


def collect(staged, parts):
    sides, tiles, _, lanes = staged.shape
    held = parts.shape[1] // sides
    for side in range(sides):
        for tile in range(tiles):
            piece = staged[side, tile].reshape(parts.shape[0], held, lanes)
            parts[:, side * held : (side + 1) * held, tile * lanes : (tile + 1) * lanes] = (
                piece.astype(parts.dtype)
            )


def scale_rows(values):
    average = jnp.mean(values, axis=0, keepdims=True)
    centered = values - average
    variance = jnp.mean(centered * centered, axis=0, keepdims=True)
    return (centered * lax.rsqrt(variance + EPS)).astype(jnp.bfloat16)


def turn(values):
    return values.astype(jnp.float32).T.astype(values.dtype)


def project(normed, weights):
    return jnp.dot(weights, normed, preferred_element_type=jnp.float32)


def stage_row(row, rows, channels, weights, mask, staged):
    projected = project(scale_rows(channels), weights)
    width = staged.shape[2] // rows
    for side in range(2):
        gates, values = (
            projected[step * width : (step + 1) * width] for step in (2 * side, 2 * side + 1)
        )
        parts = jax.nn.sigmoid(gates) * values * mask
        for tile in range(staged.shape[1]):
            staged[side, tile, pl.ds(row, width, stride=rows), :] = parts[
                :, tile * LANES : (tile + 1) * LANES
            ]


def widen(products, wide):
    devices, held, lanes = products.shape
    held = held * lanes // (wide.shape[0] * LANES)
    for tile in range(wide.shape[0]):
        half, lane = divmod(tile * LANES, lanes)
        piece = products[:, half * held : (half + 1) * held, lane : lane + LANES]
        wide[tile] = piece.astype(jnp.float32).reshape(wide.shape[1:])


def update_row(row, rows, wide, weights_out):
    width = wide.shape[1] // rows
    tiles = [wide[tile, pl.ds(row, width, stride=rows), :] for tile in range(wide.shape[0])]
    return project(scale_rows(jnp.concatenate(tiles, axis=1)), weights_out)


def open_row(row, place, chain_each, chain_all, embed, pair_act):
    same_embed, other_embed = (
        jnp.broadcast_to(embed[step : step + 1, :], (8, embed.shape[1])).T[:, 0:1]
        for step in range(2)
    )
    same = chain_all[...] == chain_each[place]
    return pair_act[row].astype(jnp.float32).T + jnp.where(same, same_embed, other_embed)


def open_kernel(
    first, crop_each, chain_each, crop_all, chain_all, embed, weights_in, pair_act, parts, staged
):
    rows = pair_act.shape[0]
    width = staged.shape[2] // rows
    weights = turn(weights_in[0][:, : 4 * width])
    crop = crop_all[...].astype(jnp.float32)
    for row in range(rows):
        place = first[0] + row
        channels = open_row(row, place, chain_each, chain_all, embed, pair_act)
        mask = crop * crop_each[place].astype(jnp.float32)
        stage_row(row, rows, channels, weights, mask, staged)
    collect(staged, parts)


def gate_of(channels, weights):
    return jax.nn.sigmoid(project(scale_rows(channels), weights))


def open_gate_kernel(first, chain_each, chain_all, embed, weights_in, pair_act, pair_sum, gate):
    weights = turn(weights_in[0][:, weights_in.shape[2] - pair_sum.shape[1] :])
    for row in range(pair_act.shape[0]):
        channels = open_row(row, first[0] + row, chain_each, chain_all, embed, pair_act)
        pair_sum[row] = channels
        gate[row] = gate_of(channels, weights)


def start_copies(source, target, sems, row):
    copies = [
        pltpu.make_async_copy(one.at[row], other.at[row], sems.at[side, row])
        for side, (one, other) in enumerate(zip(source, target))
    ]
    for copy in copies:
        copy.start()
    return copies


def middle_kernel(
    first,
    crop_each,
    crop_all,
    weights_out,
    weights_in,
    products,
    pair_from,
    gate_from,
    parts,
    pair_far,
    wide,
    staged,
    pair_sum,
    gate,
    pair_next,
    updates,
    sems,
    next_sems,
):
    rows = pair_sum.shape[0]
    width = staged.shape[2] // rows
    arriving = [
        start_copies((pair_from, gate_from), (pair_sum, gate), sems, row) for row in range(rows)
    ]
    widen(products, wide)
    weights, turned = turn(weights_in[1][:, : 4 * width]), turn(weights_out[0])
    crop = crop_all[...].astype(jnp.float32)
    for row in range(rows):
        updates[row] = update_row(row, rows, wide, turned)
    for copies in arriving:
        for copy in copies:
            copy.wait()
    for row in range(rows):
        mask = crop * crop_each[first[0] + row].astype(jnp.float32)
        channels = pair_sum[row] + gate[row] * updates[row]
        pair_next[row] = channels
        stage_row(row, rows, channels, weights, mask, staged)
    leaving = [start_copies((pair_next,), (pair_far,), next_sems, row) for row in range(rows)]
    collect(staged, parts)
    for copies in leaving:
        for copy in copies:
            copy.wait()


def middle_gate_kernel(weights_in, pair_sum, gate):
    weights = turn(weights_in[1][:, weights_in.shape[2] - pair_sum.shape[1] :])
    for row in range(pair_sum.shape[0]):
        gate[row] = gate_of(pair_sum[row], weights)


def close_kernel(
    weights_out, products, pair_from, gate_from, pair_new, wide, pair_sum, gate, updates, sems
):
    rows = pair_sum.shape[0]
    arriving = [
        start_copies((pair_from, gate_from), (pair_sum, gate), sems, row) for row in range(rows)
    ]
    widen(products, wide)
    turned = turn(weights_out[1])
    for row in range(rows):
        updates[row] = update_row(row, rows, wide, turned)
    for copies in arriving:
        for copy in copies:
            copy.wait()
    for row in range(rows):
        channels = pair_sum[row] + gate[row] * updates[row]
        pair_new[row] = channels.T.astype(pair_new.dtype)


def attend_kernel(key_bias, score_proj, value_gate, column_out, got, out, wide, staged):
    tiles, held, _ = wide.shape
    seqs = key_bias.shape[0]
    rows = held // seqs
    for tile in range(tiles):
        piece = got[:, :, tile * LANES : (tile + 1) * LANES]
        wide[tile] = piece.astype(jnp.float32).reshape(held, LANES)
    query, value, gates, last = (
        turn(weights) for weights in (score_proj[0], value_gate[0], value_gate[1], column_out[...])
    )
    bias = jnp.broadcast_to(key_bias[...], (seqs, seqs))

    def attend(row, carry):
        column = jnp.concatenate(
            [wide[tile, pl.ds(row, seqs, stride=rows), :] for tile in range(tiles)], axis=1
        )
        normed_wide = normalize(column, 1)
        normed = normed_wide.astype(jnp.bfloat16)
        turned = normed_wide.T.astype(jnp.bfloat16)
        queries = (project(turned, query) * HEAD_DIM ** (-0.5)).astype(jnp.bfloat16)
        key_rows = project(score_proj[1], normed).astype(jnp.bfloat16)
        value_rows = project(turned, value).astype(jnp.bfloat16)
        gate_rows = jax.nn.sigmoid(project(turned, gates))
        mixture = []
        for head in range(HEADS):
            span = slice(head * HEAD_DIM, (head + 1) * HEAD_DIM)
            scores = project(queries[span], key_rows[:, span]) + bias
            raised = jnp.exp(scores - jnp.max(scores, axis=0, keepdims=True))
            weights = raised * (1.0 / jnp.sum(raised, axis=0, keepdims=True))
            mixture.append(project(weights.astype(jnp.bfloat16), value_rows[span]))
        gated = (gate_rows * jnp.concatenate(mixture, axis=0)).astype(jnp.bfloat16)
        column += project(gated, last).T
        for tile in range(tiles):
            staged[tile, pl.ds(row, seqs, stride=rows), :] = column[
                :, tile * LANES : (tile + 1) * LANES
            ]
        return carry

    lax.fori_loop(0, rows, attend, 0)
    for tile in range(tiles):
        out[:, tile * LANES : (tile + 1) * LANES] = staged[tile].astype(out.dtype)


KERNEL = pltpu.CompilerParams(vmem_limit_bytes=60 * 1024 * 1024)
HERE = pl.BlockSpec(memory_space=pltpu.VMEM)
EACH = pl.BlockSpec(memory_space=pltpu.SMEM)
FAR = pl.BlockSpec(memory_space=pl.ANY)


def shapes_of(rows, side, channels, devices):
    parts = jax.ShapeDtypeStruct((devices, 2 * channels * rows // devices, side), jnp.bfloat16)
    held = jax.ShapeDtypeStruct((rows, channels, side), jnp.float32)
    tiles = (side // LANES, channels * rows, LANES)
    return (
        parts,
        held,
        pltpu.VMEM(tiles, jnp.float32),
        pltpu.VMEM((2,) + tiles, jnp.float32),
    )


def open_pair(first, crop, chains, embed, weights_in, pair_act, devices):
    parts, _, _, staged = shapes_of(*pair_act.shape, devices)
    return pl.pallas_call(
        open_kernel,
        in_specs=[EACH] * 3 + [HERE] * 5,
        out_specs=HERE,
        out_shape=parts,
        scratch_shapes=[staged],
        compiler_params=KERNEL,
    )(first, crop, chains, crop[None], chains[None], embed, weights_in, pair_act)


def open_gate(first, chains, embed, weights_in, pair_act, devices):
    _, held, _, _ = shapes_of(*pair_act.shape, devices)
    return pl.pallas_call(
        open_gate_kernel,
        in_specs=[EACH] * 2 + [HERE] * 4,
        out_specs=(HERE, HERE),
        out_shape=(held, held),
        compiler_params=KERNEL,
    )(first, chains, chains[None], embed, weights_in, pair_act)


def middle_pair(first, crop, weights_out, weights_in, products, pair_sum, gate):
    rows, channels, side = pair_sum.shape
    devices, held, lanes = products.shape
    parts, pair_next, wide, staged = shapes_of(rows, side, channels, devices)
    near = pltpu.VMEM(pair_sum.shape, jnp.float32)
    return pl.pallas_call(
        middle_kernel,
        grid=(1,),
        in_specs=[EACH] * 2
        + [HERE] * 3
        + [pl.BlockSpec((devices, held // 2, lanes), lambda step: (0, 0, 0)), FAR, FAR],
        out_specs=(HERE, FAR),
        out_shape=(parts, pair_next),
        scratch_shapes=[wide, staged, near, near, near, near]
        + [pltpu.SemaphoreType.DMA((2, rows)), pltpu.SemaphoreType.DMA((1, rows))],
        compiler_params=KERNEL,
    )(first, crop, crop[None], weights_out, weights_in, products, pair_sum, gate)


def middle_gate(weights_in, pair_sum):
    return pl.pallas_call(
        middle_gate_kernel,
        in_specs=[HERE] * 2,
        out_specs=HERE,
        out_shape=jax.ShapeDtypeStruct(pair_sum.shape, jnp.float32),
        compiler_params=KERNEL,
    )(weights_in, pair_sum)


def close_pair(weights_out, products, pair_sum, gate):
    rows, channels, side = pair_sum.shape
    _, _, wide, _ = shapes_of(rows, side, channels, products.shape[0])
    near = pltpu.VMEM(pair_sum.shape, jnp.float32)
    return pl.pallas_call(
        close_kernel,
        in_specs=[HERE] * 2 + [FAR] * 2,
        out_specs=HERE,
        out_shape=jax.ShapeDtypeStruct((rows, side, channels), jnp.bfloat16),
        scratch_shapes=[wide, near, near, near, pltpu.SemaphoreType.DMA((2, rows))],
        compiler_params=KERNEL,
    )(weights_out, products, pair_sum, gate)


def attend_columns(key_bias, score_proj, value_gate, column_out, got, rows):
    devices, held, depth = got.shape
    seqs = key_bias.shape[0]
    wide = pltpu.VMEM((depth // LANES, seqs * rows, LANES), jnp.float32)
    moves = seqs * depth * (4 * depth + 2 * seqs + depth)
    return pl.pallas_call(
        attend_kernel,
        grid=(1,),
        in_specs=[HERE] * 4 + [pl.BlockSpec((devices, held // 2, depth), lambda step: (0, 1, 0))],
        out_specs=HERE,
        out_shape=jax.ShapeDtypeStruct((seqs * rows, depth), jnp.bfloat16),
        scratch_shapes=[wide, wide],
        compiler_params=KERNEL,
        cost_estimate=pl.CostEstimate(
            flops=2 * rows * moves,
            bytes_accessed=4 * seqs * rows * depth,
            transcendentals=rows * seqs * (HEADS * seqs + depth),
        ),
    )(key_bias[:, None], score_proj, value_gate, column_out, got)


def split_parts(both, share, rows):
    devices, held, side = both.shape
    both = both.reshape(devices, 2, share, rows, side)
    return both[:, 0], both[:, 1]


def block_products(products, devices, lanes):
    share, side, _ = products.shape
    blocks = products.reshape(share, devices, side // devices, side // lanes, lanes)
    return blocks.transpose(1, 3, 0, 2, 4).reshape(devices, -1, lanes)


def exchange_blocks(blocks):
    return lax.all_to_all(blocks, "dap", split_axis=0, concat_axis=0, tiled=True)


def on_device(
    alignment,
    pair_act,
    crop_mask,
    seq_mask,
    chain_ids,
    chain_embed,
    score_proj,
    value_gate,
    column_out,
    triangle_in,
    triangle_out,
):
    rows_here = pair_act.shape[0]
    width = triangle_out.shape[1]
    devices = lax.axis_size("dap")
    row_start = lax.axis_index("dap") * rows_here
    share = width // devices
    seq_here, _, depth = alignment.shape
    sent = alignment.reshape(seq_here, devices, rows_here, depth)
    sent = jnp.moveaxis(sent, 1, 0).reshape(devices, -1, depth)
    carrier = jnp.concatenate([jnp.zeros_like(sent), sent], axis=1)

    kept_rows = jnp.maximum(seq_mask, (jnp.arange(seq_mask.shape[0]) == 0).astype(jnp.int32))
    key_bias = (kept_rows - 1).astype(jnp.float32) * 1000000000.0
    first_row = row_start.reshape(1).astype(jnp.int32)
    parts = open_pair(
        first_row, crop_mask, chain_ids, chain_embed, triangle_in, pair_act, devices
    )
    both = exchange_blocks(parts)
    pair_sum, gate = open_gate(first_row, chain_ids, chain_embed, triangle_in, pair_act, devices)
    both, carrier, pair_sum, gate = lax.optimization_barrier((both, carrier, pair_sum, gate))
    left, right = split_parts(both, share, rows_here)
    left = jnp.moveaxis(left, 1, 0).reshape(share, -1, left.shape[-1])
    right = jnp.moveaxis(right, 1, 0).reshape(share, -1, right.shape[-1])
    products = jnp.einsum(
        "cik,cjk->cij", left, right, preferred_element_type=jnp.float32
    ).astype(jnp.bfloat16)
    products = block_products(products, devices, depth)
    got = exchange_blocks(lax.dynamic_update_slice(carrier, products, (0, 0, 0)))
    parts, pair_sum = middle_pair(
        first_row, crop_mask, triangle_out, triangle_in, got, pair_sum, gate
    )
    parts, got = lax.optimization_barrier((parts, got))
    both = exchange_blocks(parts)
    attended = attend_columns(key_bias, score_proj, value_gate, column_out, got, rows_here)
    both, attended, pair_sum = lax.optimization_barrier((both, attended, pair_sum))
    left, right = split_parts(both, share, rows_here)
    left = jnp.moveaxis(left, 1, 0).reshape(share, -1, left.shape[-1])
    right = jnp.moveaxis(right, 1, 0).reshape(share, -1, right.shape[-1])
    products = jnp.einsum(
        "cki,ckj->cij", left, right, preferred_element_type=jnp.float32
    ).astype(jnp.bfloat16)
    products = exchange_blocks(block_products(products, devices, products.shape[-1]))
    gate = middle_gate(triangle_in, pair_sum)
    alignment_new = attended.reshape(-1, rows_here, depth)
    products, gate = lax.optimization_barrier((products, gate))
    pair_new = close_pair(triangle_out, products, pair_sum, gate)
    return (alignment_new, pair_new)


def solution(mesh):
    placed = (
        P(("dp", "dap"), None, None),
        P(("dp", "dap"), None, None),
        P("dp"),
        P("dp"),
        P("dp"),
        P(),
        P(),
        P(),
        P(),
        P(),
        P(),
    )
    return jax.shard_map(
        on_device,
        mesh=mesh,
        in_specs=placed,
        out_specs=(P("dp", "dap", None), P(("dp", "dap"), None, None)),
        check_vma=False,
    )
```
